256 devices in a mesh: dp: 32 (over x, z), ctx: 8 (over y, core).
Axes of the slice: x: 4, y: 4, z: 8, core: 2. Of those that a mesh axis runs over, the one named last changes fastest.
Arguments:
- queries: bfloat16 [128, 512, 2048], P('dp', 'ctx'), may hold values from -72 to 72
- keyvals: bfloat16 [128, 512, 1024], P('dp', 'ctx'), may hold values from -6 to 6
- segments: int32 [128, 512], replicated, may hold values from 0 to 3, never falling along the last dimension, each value on 1 to 256 neighbouring positions
- plan: int32 [128], replicated, may hold values from 0 to 127, as said below
Outputs:
- attended: bfloat16 [128, 512, 2048], P('dp', 'ctx')
The draws below stay inside these ranges and needn't reach their ends.
Inputs may be any that keep to these rules, and one draw needn't show every extreme that they name: plan is a permutation; every data rank receives 4 packs, no data rank sends more than 1 packs to one data rank, and some pairs of ranks reach that.
All inputs are finite; a program needn't handle non-finite values.
Results may differ from the reference program's by a relative error of at most 0.01.
Values may be sent and summed in bfloat16 or wider, within the bound.
A program may use at most 64 MiB of HBM per device.

```python
import math
import jax
import jax.numpy as jnp
import numpy as np
from jax import lax

HEADS = 32
KV_HEADS = 8
HEAD_DIM = 64
PACK = 512
PACKS = 4
DOCS = 4
PACKS_ALL = 128


def draw_queries(key, part):
    key = jax.random.fold_in(key, 7)
    result = jnp.clip(jax.random.normal(key, (PACKS_ALL, PACK, HEADS, HEAD_DIM), jnp.float32), -6.0, 6.0)
    return result.reshape(PACKS_ALL, PACK, HEADS * HEAD_DIM).astype(jnp.bfloat16)


def draw_keyvals(key, part):
    key = jax.random.fold_in(key, 13)
    val_key = jax.random.fold_in(key, 11)
    key_part = jnp.clip(jax.random.normal(key, (PACKS_ALL, PACK, KV_HEADS, HEAD_DIM), jnp.float32), -6.0, 6.0)
    val_part = jnp.clip(jax.random.normal(val_key, (PACKS_ALL, PACK, KV_HEADS, HEAD_DIM), jnp.float32), -6.0, 6.0)
    stacked = jnp.stack([key_part, val_part], axis=3)
    return stacked.reshape(PACKS_ALL, PACK, 2 * KV_HEADS * HEAD_DIM).astype(jnp.bfloat16)


def draw_plan(key, part):
    key = jax.random.fold_in(key, 5)
    key_a, key_b, key_c = jax.random.split(key, 3)
    rank_count = PACKS_ALL // PACKS
    line_up = jax.random.permutation(key_a, rank_count).astype(jnp.int32)
    place_of = jnp.zeros((rank_count,), jnp.int32).at[line_up].set(jnp.arange(rank_count, dtype=jnp.int32))
    shifts = jax.random.permutation(key_b, rank_count).astype(jnp.int32)[jnp.arange(PACKS) % rank_count]
    turn_of = jax.random.randint(key_c, (rank_count,), 0, PACKS)
    sender = jnp.arange(rank_count)
    target = line_up[(place_of[sender][:, None] + shifts[None, :]) % rank_count]
    slot_at = (jnp.arange(PACKS)[None, :] + turn_of[target]) % PACKS
    return (target * PACKS + slot_at).reshape(-1).astype(jnp.int32)


def length_profile(amount, total, most, slope):
    weights = [(1 << 20) // math.isqrt(rank ** slope) + 1 for rank in range(2, amount + 1)]
    spare, counts = total - most - (amount - 1), [1] * (amount - 1)
    while spare > 0:
        free = [i for i in range(amount - 1) if counts[i] < most]
        mass, remaining = sum([weights[i] for i in free]), spare
        for i in free:
            extra = min(most - counts[i], max(1, remaining * weights[i] // mass), spare)
            counts[i] = counts[i] + extra
            spare = spare - extra
    return np.array([most] + counts)


def uneven_parts(own_key, amount, total, limit, slope):
    if amount == 2:
        one = jax.random.randint(own_key, (), max(1, total - limit), min(limit, total - 1) + 1)
        return jnp.stack([one, total - one])
    lengths = jnp.asarray(length_profile(amount, total, limit, slope), jnp.int32)
    pairs = (amount - 1) // 2
    source_of, receiver = lengths[1:1 + 2 * pairs:2], lengths[2:2 + 2 * pairs:2]
    slack = jnp.minimum(source_of - 1, limit - receiver)
    passed = jax.random.randint(jax.random.fold_in(own_key, 1), (pairs,), 0, 1 << 20) % (slack + 1)
    lengths = lengths.at[1:1 + 2 * pairs:2].set(source_of - passed).at[2:2 + 2 * pairs:2].set(receiver + passed)
    return lengths[jax.random.permutation(jax.random.fold_in(own_key, 2), amount)]


def setup_inputs(seed: int = 0) -> dict:
    keys = jax.random.split(jax.random.key(seed), 5)
    return {
        "queries": draw_queries(jax.random.fold_in(keys[4], 71), 0),
        "keyvals": draw_keyvals(jax.random.fold_in(keys[4], 71), 0),
        "segments": jax.vmap(lambda own: jnp.searchsorted(jnp.cumsum(uneven_parts(own, DOCS, PACK, PACK // 2, 1)), jnp.arange(PACK), side="right"))(jax.random.split(keys[2], PACKS_ALL)).reshape((PACKS_ALL, PACK)).astype(jnp.int32),
        "plan": draw_plan(jax.random.fold_in(keys[4], 71), 0),
    }


def attend_pack(q_pack, kv_pack, seg_pack):
    length = q_pack.shape[0]
    group_size = HEADS // KV_HEADS
    q_heads = q_pack.astype(jnp.float32).reshape(length, KV_HEADS, group_size, HEAD_DIM)
    kv_heads = kv_pack.astype(jnp.float32).reshape(length, KV_HEADS, 2, HEAD_DIM)
    scores = jnp.einsum("qhgd,khd->hgqk", q_heads, kv_heads[:, :, 0]) * (HEAD_DIM ** -0.5)
    pos_ids = jnp.arange(length, dtype=jnp.int32)
    allowed = (seg_pack[:, None] == seg_pack[None, :]) & (pos_ids[None, :] <= pos_ids[:, None])
    scores = jnp.where(allowed, scores, jnp.float32(-1e30))
    row_max = jnp.max(scores, axis=-1, keepdims=True)
    exp_sc = jnp.exp(scores - row_max)
    weights = (exp_sc / jnp.sum(exp_sc, axis=-1, keepdims=True)).astype(jnp.bfloat16)
    mixed_out = jnp.einsum("hgqk,khd->qhgd", weights.astype(jnp.float32), kv_heads[:, :, 1])
    return mixed_out.astype(jnp.bfloat16).reshape(length, HEADS * HEAD_DIM)


def reference(queries, keyvals, segments, plan):
    pack_total = plan.shape[0]
    source = jnp.zeros((pack_total,), jnp.int32).at[plan.astype(jnp.int32)].set(jnp.arange(pack_total, dtype=jnp.int32))

    def one_dest(src_pack):
        return attend_pack(queries[src_pack], keyvals[src_pack], segments[src_pack])

    return lax.map(one_dest, source)
```

```python
import functools

import jax
import jax.numpy as jnp
from jax import lax
from jax.experimental import pallas as pl
from jax.experimental.pallas import tpu as pltpu
from jax.sharding import PartitionSpec as P

MESH = pl.DeviceIdType.MESH
HEAD = 64
PACK = 512
PACKS = 4
ALL = 128
XN, ZN, CTX = 4, 8, 8
RANKS = XN * ZN
ROWS = PACK // CTX
SUB = ROWS // XN
LANES = 128
QB = 128
WINDOW = 384
NEG = -1e30
EXP2_SCALE = HEAD**-0.5 * 1.4426950408889634
NN = (((1,), (0,)), ((), ()))
NT = (((1,), (1,)), ((), ()))


def make_bias(seg_ref, row, bias, i):
    seg_row = seg_ref[pl.ds(row, 1), :]
    lower = lax.broadcasted_iota(jnp.int32, (QB, QB), 1) <= lax.broadcasted_iota(jnp.int32, (QB, QB), 0)
    for b in range(PACK // QB):
        seg_q = jnp.transpose(jnp.broadcast_to(seg_row[:, b * QB : (b + 1) * QB], (QB, QB)))
        first = max(0, b - 2)
        for kb in range(first, b + 1):
            seg_k = jnp.broadcast_to(seg_row[:, kb * QB : (kb + 1) * QB], (QB, QB))
            same = seg_q == seg_k
            if kb == b:
                same = same & lower
            bias[i, b * QB : (b + 1) * QB, (kb - first) * QB : (kb - first + 1) * QB] = jnp.where(same, 0.0, NEG)


def attend(q_c, kvf, bias, att_c, i):
    kv = kvf[i].astype(jnp.float32)
    swapped = pltpu.roll(kv, HEAD, 1)
    left = lax.broadcasted_iota(jnp.int32, (PACK, LANES), 1) < HEAD
    keys = (
        jnp.where(left, kv, 0.0).astype(jnp.bfloat16),
        jnp.where(left, 0.0, swapped).astype(jnp.bfloat16),
    )
    values = (
        jnp.where(left, swapped, 1.0).astype(jnp.bfloat16),
        jnp.where(left, 1.0, kv).astype(jnp.bfloat16),
    )
    left_q = lax.broadcasted_iota(jnp.int32, (QB, LANES), 1) < HEAD
    for b in range(PACK // QB):
        lo, hi = max(0, b - 2) * QB, (b + 1) * QB
        q = q_c[i, b * QB : hi, :]
        mask = bias[i, b * QB : hi, 0 : hi - lo]
        sums = []
        for h in range(2):
            s = lax.dot_general(q, keys[h][lo:hi], NT, preferred_element_type=jnp.float32) + mask
            top = jnp.max(s, axis=1, keepdims=True)
            p = jnp.exp2((s - top) * EXP2_SCALE).astype(jnp.bfloat16)
            sums.append(lax.dot_general(p, values[h][lo:hi], NN, preferred_element_type=jnp.float32))
        total = jnp.where(left_q, sums[0], sums[1])
        norm = pltpu.roll(jnp.where(left_q, sums[1], sums[0]), HEAD, 1)
        att_c[i, b * QB : hi, :] = (total / norm).astype(jnp.bfloat16)


def kernel(
    inv_ref, seg_ref, q_ref, kv_ref, out_ref,
    kvf, bias, qf0, qf1, att0, att1, mid0, mid1, snd0, snd1,
    kv_recv, q_recv, p1_send, mid_recv, mid_send, out_recv, out_send,
):
    rank, ctx = lax.axis_index("dp"), lax.axis_index("ctx")
    xs, zs = rank // ZN, rank % ZN
    qf, att, mid, snd = (qf0, qf1), (att0, att1), (mid0, mid1), (snd0, snd1)
    my_rows = pl.ds(pl.multiple_of(ctx * ROWS, ROWS), ROWS)

    def kv_cols(i, g):
        return kv_ref.at[i, :, pl.ds(pl.multiple_of(g * LANES, LANES), LANES)]

    def q_cols(i, g, c):
        return q_ref.at[i, :, pl.ds(pl.multiple_of(g * 2 * LANES + c * LANES, LANES), LANES)]

    def remote(src, dst, send, recv, to):
        pltpu.make_async_remote_copy(
            src_ref=src, dst_ref=dst, send_sem=send, recv_sem=recv, device_id=to, device_id_type=MESH
        ).start()

    def await_bytes(ref, sem):
        pltpu.make_async_copy(ref, ref, sem).wait()

    def give_kv_q0(n, _):
        i, g = n // (CTX - 1), (ctx + 1 + n % (CTX - 1)) % CTX
        remote(kv_cols(i, g), kvf.at[i, my_rows], p1_send.at[0], kv_recv.at[i], (rank, g))
        remote(q_cols(i, g, 0), qf0.at[i, my_rows], p1_send.at[1], q_recv.at[0, i], (rank, g))
        return 0

    def give_q1(n, _):
        i, g = n // (CTX - 1), (ctx + 1 + n % (CTX - 1)) % CTX
        remote(q_cols(i, g, 1), qf1.at[i, my_rows], p1_send.at[2], q_recv.at[1, i], (rank, g))
        return 0

    for i in range(PACKS):
        pltpu.make_async_copy(kv_cols(i, ctx), kvf.at[i, my_rows], kv_recv.at[i]).start()
        for c in range(2):
            pltpu.make_async_copy(q_cols(i, ctx, c), qf[c].at[i, my_rows], q_recv.at[c, i]).start()
    lax.fori_loop(0, PACKS * (CTX - 1), give_kv_q0, 0)
    lax.fori_loop(0, PACKS * (CTX - 1), give_q1, 0)

    def spread(c):
        def one(n, _):
            x, t = (xs + n // CTX) % XN, (ctx + n % CTX) % CTX
            to = x * ZN + (ctx + t) % ZN
            here = (to == rank) & (t == ctx)
            src = att[c].at[:, pl.ds(pl.multiple_of(t * ROWS + x * SUB, SUB), SUB), :]
            dst = mid[c].at[pl.ds(rank * PACKS, PACKS)]

            @pl.when(here)
            def _():
                pltpu.make_async_copy(src, dst, mid_recv.at[c]).start()

            @pl.when(jnp.logical_not(here))
            def _():
                remote(src, dst, mid_send.at[c], mid_recv.at[c], (to, t))

            return 0

        lax.fori_loop(0, RANKS, one, 0)

    for c in range(2):

        def work(i, _):
            if c == 0:
                await_bytes(kvf.at[i], kv_recv.at[i])
                make_bias(seg_ref, rank * PACKS + i, bias, i)
            await_bytes(qf[c].at[i], q_recv.at[c, i])
            attend(qf[c], kvf, bias, att[c], i)
            return 0

        lax.fori_loop(0, PACKS, work, 0)
        spread(c)

    head = (zs - ctx + ZN) % ZN

    for c in range(2):
        await_bytes(mid[c], mid_recv.at[c])

        def deliver(n, _):
            to = (xs + n // ZN) % XN * ZN + (zs + n % ZN) % ZN
            for j in range(PACKS):
                snd[c][to * PACKS + j] = mid[c][inv_ref[to * PACKS + j]]
            src = snd[c].at[pl.ds(to * PACKS, PACKS)]
            dst = out_ref.at[
                :,
                pl.ds(pl.multiple_of(xs * SUB, SUB), SUB),
                pl.ds(pl.multiple_of(head * 2 * LANES + c * LANES, LANES), LANES),
            ]

            @pl.when(to == rank)
            def _():
                pltpu.make_async_copy(src, dst, out_recv).start()

            @pl.when(to != rank)
            def _():
                remote(src, dst, out_send.at[c], out_recv, (to, ctx))

            return 0

        lax.fori_loop(0, RANKS, deliver, 0)

    await_bytes(kvf.at[:, 0 : PACK - ROWS], p1_send.at[0])
    await_bytes(qf0.at[:, 0 : PACK - ROWS], p1_send.at[1])
    await_bytes(qf1.at[:, 0 : PACK - ROWS], p1_send.at[2])
    keeps_one = (2 * ctx) % ZN == zs
    for c in range(2):

        @pl.when(keeps_one)
        def _():
            await_bytes(mid[c].at[0 : ALL - PACKS], mid_send.at[c])

        @pl.when(jnp.logical_not(keeps_one))
        def _():
            await_bytes(mid[c], mid_send.at[c])

        await_bytes(snd[c].at[0 : ALL - PACKS], out_send.at[c])
    await_bytes(out_ref, out_recv)


def per_device(queries, keyvals, segments, plan):
    order = jnp.arange(ALL, dtype=jnp.int32)
    inverse = jnp.sum(jnp.where(plan[:, None] == order[None, :], order[:, None], 0), axis=0)
    full = (PACKS, PACK, LANES)
    pieces = (ALL, SUB, LANES)
    dma = pltpu.SemaphoreType.DMA
    return pl.pallas_call(
        kernel,
        out_shape=jax.ShapeDtypeStruct((PACKS, ROWS, queries.shape[2]), jnp.bfloat16),
        in_specs=[
            pl.BlockSpec(memory_space=pltpu.SMEM),
            pl.BlockSpec(memory_space=pltpu.VMEM),
            pl.BlockSpec(memory_space=pl.ANY),
            pl.BlockSpec(memory_space=pl.ANY),
        ],
        out_specs=pl.BlockSpec(memory_space=pl.ANY),
        scratch_shapes=[
            pltpu.VMEM(full, jnp.bfloat16),
            pltpu.VMEM((PACKS, PACK, WINDOW), jnp.float32),
            *[pltpu.VMEM(full, jnp.bfloat16)] * 4,
            *[pltpu.VMEM(pieces, jnp.bfloat16)] * 4,
            dma((PACKS,)),
            dma((2, PACKS)),
            dma((3,)),
            dma((2,)),
            dma((2,)),
            dma(()),
            dma((2,)),
        ],
        compiler_params=pltpu.CompilerParams(has_side_effects=True, vmem_limit_bytes=24 * 2**20),
        cost_estimate=pl.CostEstimate(flops=2 * 10**9, bytes_accessed=4 * 2**20, transcendentals=2 * 10**6),
    )(inverse, segments, queries, keyvals)


def solution(mesh):
    return jax.shard_map(
        per_device,
        mesh=mesh,
        in_specs=(P("dp", "ctx", None), P("dp", "ctx", None), P(), P()),
        out_specs=P("dp", "ctx", None),
        check_vma=False,
    )
```

```python
import functools

import jax
import jax.numpy as jnp
from jax import lax
from jax.experimental import pallas as pl
from jax.experimental.pallas import tpu as pltpu
from jax.sharding import PartitionSpec as P

MESH = pl.DeviceIdType.MESH
HEAD = 64
PACK = 512
PACKS = 4
ALL = 128
XN, ZN, CTX = 4, 8, 8
RANKS = XN * ZN
AHEAD = 4
ROWS = PACK // CTX
SUB = ROWS // XN
LANES = 128
QB = 128
WINDOW = 384
NEG = -1e30
EXP2_SCALE = HEAD**-0.5 * 1.4426950408889634
NN = (((1,), (0,)), ((), ()))
NT = (((1,), (1,)), ((), ()))


def make_bias(seg_ref, row, bias, i):
    seg_row = seg_ref[pl.ds(row, 1), :]
    lower = lax.broadcasted_iota(jnp.int32, (QB, QB), 1) <= lax.broadcasted_iota(jnp.int32, (QB, QB), 0)
    for b in range(PACK // QB):
        seg_q = jnp.transpose(jnp.broadcast_to(seg_row[:, b * QB : (b + 1) * QB], (QB, QB)))
        first = max(0, b - 2)
        for kb in range(first, b + 1):
            seg_k = jnp.broadcast_to(seg_row[:, kb * QB : (kb + 1) * QB], (QB, QB))
            same = seg_q == seg_k
            if kb == b:
                same = same & lower
            bias[i, b * QB : (b + 1) * QB, (kb - first) * QB : (kb - first + 1) * QB] = jnp.where(same, 0.0, NEG)


def attend(q_c, kvf, bias, att_c, i):
    kv = kvf[i].astype(jnp.float32)
    swapped = pltpu.roll(kv, HEAD, 1)
    left = lax.broadcasted_iota(jnp.int32, (PACK, LANES), 1) < HEAD
    keys = (
        jnp.where(left, kv, 0.0).astype(jnp.bfloat16),
        jnp.where(left, 0.0, swapped).astype(jnp.bfloat16),
    )
    values = (
        jnp.where(left, swapped, 1.0).astype(jnp.bfloat16),
        jnp.where(left, 1.0, kv).astype(jnp.bfloat16),
    )
    left_q = lax.broadcasted_iota(jnp.int32, (QB, LANES), 1) < HEAD
    for b in range(PACK // QB):
        lo, hi = max(0, b - 2) * QB, (b + 1) * QB
        q = q_c[i, b * QB : hi, :]
        mask = bias[i, b * QB : hi, 0 : hi - lo]
        sums = []
        for h in range(2):
            s = lax.dot_general(q, keys[h][lo:hi], NT, preferred_element_type=jnp.float32) + mask
            top = jnp.max(s, axis=1, keepdims=True)
            p = jnp.exp2((s - top) * EXP2_SCALE).astype(jnp.bfloat16)
            sums.append(lax.dot_general(p, values[h][lo:hi], NN, preferred_element_type=jnp.float32))
        total = jnp.where(left_q, sums[0], sums[1])
        norm = pltpu.roll(jnp.where(left_q, sums[1], sums[0]), HEAD, 1)
        att_c[i, b * QB : hi, :] = (total / norm).astype(jnp.bfloat16)


def kernel(
    plan_ref, seg_ref, q_ref, kv_ref, out_ref,
    kvf, bias, qf0, qf1, att0, att1, mid0, mid1, snd0, snd1, segs, inv_row, inv_ref, q_v, kv_v,
    kv_recv, q_recv, p1_send, mid_recv, mid_send, out_recv, out_send, small, group_in, all_in,
):
    rank, ctx = lax.axis_index("dp"), lax.axis_index("ctx")
    xs, zs = rank >> 3, rank & 7
    qf, att, mid, snd = (qf0, qf1), (att0, att1), (mid0, mid1), (snd0, snd1)
    my_rows = pl.ds(pl.multiple_of(ctx * ROWS, ROWS), ROWS)

    def kv_cols(i, g):
        return kv_v.at[i, :, pl.ds(pl.multiple_of(g * LANES, LANES), LANES)]

    def q_cols(i, g, c):
        return q_v.at[i, :, pl.ds(pl.multiple_of(g * 2 * LANES + c * LANES, LANES), LANES)]

    def remote(src, dst, send, recv, to):
        pltpu.make_async_remote_copy(
            src_ref=src, dst_ref=dst, send_sem=send, recv_sem=recv, device_id=to, device_id_type=MESH
        ).start()

    def await_bytes(ref, sem):
        pltpu.make_async_copy(ref, ref, sem).wait()

    def tell(sem, to):
        pl.semaphore_signal(sem, inc=1, device_id=to, device_id_type=MESH)

    def give_kv_q0(i):
        def one(n, _):
            g = (ctx + n) & 7
            remote(kv_cols(i, g), kvf.at[i, my_rows], p1_send.at[0], kv_recv.at[i], (rank, g))
            remote(q_cols(i, g, 0), qf0.at[i, my_rows], p1_send.at[1], q_recv.at[0, i], (rank, g))
            return 0

        for n in range(1, CTX):
            one(n, 0)

    def give_q1(i):
        def one(n, _):
            g = (ctx + n) & 7
            remote(q_cols(i, g, 1), qf1.at[i, my_rows], p1_send.at[2], q_recv.at[1, i], (rank, g))
            return 0

        for n in range(1, CTX):
            one(n, 0)

    barrier = pltpu.get_barrier_semaphore()

    @pl.when(ctx != 0)
    def _():
        tell(barrier, (rank, 0))

    first = pl.multiple_of((rank >> 1) * 2 * PACKS, 2 * PACKS)
    seg_copy = pltpu.make_async_copy(seg_ref.at[pl.ds(first, 2 * PACKS)], segs, small.at[0])
    seg_copy.start()
    own = (pltpu.make_async_copy(kv_ref, kv_v, small.at[2]), pltpu.make_async_copy(q_ref, q_v, small.at[3]))
    for copy in own:
        copy.start()

    @pl.when(ctx == 0)
    def _():
        pl.semaphore_wait(barrier, CTX - 1)
        lax.fori_loop(1, CTX, lambda m, _: (tell(group_in, (rank, m)), 0)[1], 0)

    @pl.when(ctx != 0)
    def _():
        pl.semaphore_wait(group_in, 1)

    for copy in own:
        copy.wait()
    for i in range(AHEAD):
        give_kv_q0(i)
    for i in range(PACKS):
        pltpu.make_async_copy(kv_cols(i, ctx), kvf.at[i, my_rows], kv_recv.at[i]).start()
        for c in range(2):
            pltpu.make_async_copy(q_cols(i, ctx, c), qf[c].at[i, my_rows], q_recv.at[c, i]).start()

    @pl.when(ctx == 0)
    def _():
        lax.fori_loop(0, RANKS, lambda m, _: (tell(barrier, ((rank + m) & 31, 1)), 0)[1], 0)


    place = jnp.transpose(jnp.broadcast_to(plan_ref[...], (ALL, ALL)))
    wanted = lax.broadcasted_iota(jnp.int32, (ALL, ALL), 1)
    source = lax.broadcasted_iota(jnp.int32, (ALL, ALL), 0)
    inv_row[...] = jnp.max(jnp.where(place == wanted, source, 0), axis=0, keepdims=True)
    inv_copy = pltpu.make_async_copy(inv_row, inv_ref, small.at[1])
    inv_copy.start()
    seg_copy.wait()

    @pl.when(ctx == 1)
    def _():
        pl.semaphore_wait(barrier, RANKS)
        lax.fori_loop(1, CTX, lambda m, _: (tell(all_in, (rank, (1 + m) & 7)), 0)[1], 0)

    def spread(c, i):
        dst = mid[c].at[rank * PACKS + i]

        def row(m, _):
            x = (xs + m) & 3
            for n in range(ZN):
                z = (zs + n) & 7
                block = ((z + ctx) & 7) * XN + x
                src = att[c].at[i, pl.ds(pl.multiple_of(block * SUB, SUB), SUB), :]
                if n:
                    remote(src, dst, mid_send.at[c], mid_recv.at[c], (x * ZN + z, ctx))
                else:

                    @pl.when(m == 0)
                    def _():
                        pltpu.make_async_copy(src, dst, mid_recv.at[c]).start()

                    @pl.when(m != 0)
                    def _():
                        remote(src, dst, mid_send.at[c], mid_recv.at[c], (x * ZN + z, ctx))

            return 0

        lax.fori_loop(0, XN, row, 0)

    for c in range(2):

        def work(i, _):
            if c == 0:
                await_bytes(kvf.at[i], kv_recv.at[i])
                make_bias(segs, (rank & 1) * PACKS + i, bias, i)
            await_bytes(qf[c].at[i], q_recv.at[c, i])
            attend(qf[c], kvf, bias, att[c], i)
            if c == 0:

                @pl.when((ctx != 1) & (i == 0))
                def _():
                    pl.semaphore_wait(all_in, 1)

            spread(c, i)
            later = i + AHEAD

            @pl.when(later < PACKS)
            def _():
                (give_kv_q0, give_q1)[c](later)

            if c == 0:

                @pl.when(later >= PACKS)
                def _():
                    give_q1(later - PACKS)

            return 0

        lax.fori_loop(0, PACKS, work, 0)

    inv_copy.wait()
    to_ctx = (zs + ctx) & 7

    for c in range(2):
        await_bytes(mid[c], mid_recv.at[c])

        dst = out_ref.at[
            :,
            pl.ds(pl.multiple_of(xs * SUB, SUB), SUB),
            pl.ds(pl.multiple_of(ctx * 2 * LANES + c * LANES, LANES), LANES),
        ]

        def deliver(m, _):
            for n in range(ZN):
                to = ((xs + m) & 3) * ZN + ((zs + n) & 7)
                for j in range(PACKS):
                    snd[c][to * PACKS + j] = mid[c][inv_ref[0, to * PACKS + j]]
                src = snd[c].at[pl.ds(to * PACKS, PACKS)]
                if n:
                    remote(src, dst, out_send.at[c], out_recv, (to, to_ctx))
                else:

                    here = (m == 0) & (zs == 0)

                    @pl.when(here)
                    def _():
                        pltpu.make_async_copy(src, dst, out_recv).start()

                    @pl.when(jnp.logical_not(here))
                    def _():
                        remote(src, dst, out_send.at[c], out_recv, (to, to_ctx))

            return 0

        lax.fori_loop(0, XN, deliver, 0)

    await_bytes(kvf.at[:, 0 : PACK - ROWS], p1_send.at[0])
    await_bytes(qf0.at[:, 0 : PACK - ROWS], p1_send.at[1])
    await_bytes(qf1.at[:, 0 : PACK - ROWS], p1_send.at[2])
    for c in range(2):
        await_bytes(mid[c].at[0 : ALL - PACKS], mid_send.at[c])

        @pl.when(zs == 0)
        def _():
            await_bytes(snd[c].at[0 : ALL - PACKS], out_send.at[c])

        @pl.when(zs != 0)
        def _():
            await_bytes(snd[c], out_send.at[c])

    await_bytes(out_ref, out_recv)


def per_device(queries, keyvals, segments, plan):
    full = (PACKS, PACK, LANES)
    pieces = (ALL, SUB, LANES)
    dma = pltpu.SemaphoreType.DMA
    return pl.pallas_call(
        kernel,
        out_shape=jax.ShapeDtypeStruct((PACKS, ROWS, queries.shape[2]), jnp.bfloat16),
        in_specs=[
            pl.BlockSpec(memory_space=pltpu.VMEM),
            pl.BlockSpec(memory_space=pl.ANY),
            pl.BlockSpec(memory_space=pl.ANY),
            pl.BlockSpec(memory_space=pl.ANY),
        ],
        out_specs=pl.BlockSpec(memory_space=pl.ANY),
        scratch_shapes=[
            pltpu.VMEM(full, jnp.bfloat16),
            pltpu.VMEM((PACKS, PACK, WINDOW), jnp.float32),
            *[pltpu.VMEM(full, jnp.bfloat16)] * 4,
            *[pltpu.VMEM(pieces, jnp.bfloat16)] * 4,
            pltpu.VMEM((2 * PACKS, PACK), jnp.int32),
            pltpu.VMEM((1, ALL), jnp.int32),
            pltpu.SMEM((1, ALL), jnp.int32),
            pltpu.VMEM(queries.shape, jnp.bfloat16),
            pltpu.VMEM(keyvals.shape, jnp.bfloat16),
            dma((PACKS,)),
            dma((2, PACKS)),
            dma((3,)),
            dma((2,)),
            dma((2,)),
            dma(()),
            dma((2,)),
            dma((4,)),
            pltpu.SemaphoreType.REGULAR,
            pltpu.SemaphoreType.REGULAR,
        ],
        compiler_params=pltpu.CompilerParams(collective_id=0, has_side_effects=True, vmem_limit_bytes=60 * 2**20),
        cost_estimate=pl.CostEstimate(flops=2 * 10**9, bytes_accessed=4 * 2**20, transcendentals=2 * 10**6),
    )(plan.reshape(1, ALL), segments, queries, keyvals)


def solution(mesh):
    return jax.shard_map(
        per_device,
        mesh=mesh,
        in_specs=(P("dp", "ctx", None), P("dp", "ctx", None), P(), P()),
        out_specs=P("dp", "ctx", None),
        check_vma=False,
    )
```

```python
import functools

import jax
import jax.numpy as jnp
from jax import lax
from jax.experimental import pallas as pl
from jax.experimental.pallas import tpu as pltpu
from jax.sharding import PartitionSpec as P

MESH = pl.DeviceIdType.MESH
HEAD = 64
PACK = 512
PACKS = 4
ALL = 128
XN, ZN, CTX = 4, 8, 8
RANKS = XN * ZN
AHEAD = 4
ROWS = PACK // CTX
SUB = ROWS // XN
LANES = 128
QB = 128
WINDOW = 384
NEG = -1e30
EXP2_SCALE = HEAD**-0.5 * 1.4426950408889634
NN = (((1,), (0,)), ((), ()))
NT = (((1,), (1,)), ((), ()))


def make_bias(seg_ref, row, bias, i):
    seg_row = seg_ref[pl.ds(row, 1), :]
    lower = lax.broadcasted_iota(jnp.int32, (QB, QB), 1) <= lax.broadcasted_iota(jnp.int32, (QB, QB), 0)
    for b in range(PACK // QB):
        seg_q = jnp.transpose(jnp.broadcast_to(seg_row[:, b * QB : (b + 1) * QB], (QB, QB)))
        first = max(0, b - 2)
        for kb in range(first, b + 1):
            seg_k = jnp.broadcast_to(seg_row[:, kb * QB : (kb + 1) * QB], (QB, QB))
            same = seg_q == seg_k
            if kb == b:
                same = same & lower
            bias[i, b * QB : (b + 1) * QB, (kb - first) * QB : (kb - first + 1) * QB] = jnp.where(same, 0.0, NEG)


def prepare(kvf, keys, values, i):
    kv = kvf[i].astype(jnp.float32)
    swapped = pltpu.roll(kv, HEAD, 1)
    left = lax.broadcasted_iota(jnp.int32, (PACK, LANES), 1) < HEAD
    keys[0, i] = jnp.where(left, kv, 0.0).astype(jnp.bfloat16)
    keys[1, i] = jnp.where(left, 0.0, swapped).astype(jnp.bfloat16)
    values[0, i] = jnp.where(left, swapped, 1.0).astype(jnp.bfloat16)
    values[1, i] = jnp.where(left, 1.0, kv).astype(jnp.bfloat16)


def attend(q_c, keys, values, bias, att_c, i):
    left_q = lax.broadcasted_iota(jnp.int32, (QB, LANES), 1) < HEAD
    for b in range(PACK // QB):
        lo, hi = max(0, b - 2) * QB, (b + 1) * QB
        q = q_c[i, b * QB : hi, :]
        mask = bias[i, b * QB : hi, 0 : hi - lo]
        sums = []
        for h in range(2):
            s = lax.dot_general(q, keys[h, i, lo:hi, :], NT, preferred_element_type=jnp.float32) + mask
            top = jnp.max(s, axis=1, keepdims=True)
            p = jnp.exp2((s - top) * EXP2_SCALE).astype(jnp.bfloat16)
            sums.append(lax.dot_general(p, values[h, i, lo:hi, :], NN, preferred_element_type=jnp.float32))
        total = jnp.where(left_q, sums[0], sums[1])
        norm = pltpu.roll(jnp.where(left_q, sums[1], sums[0]), HEAD, 1)
        att_c[i, b * QB : hi, :] = (total / norm).astype(jnp.bfloat16)


def kernel(
    plan_ref, seg_ref, q_ref, kv_ref, out_ref,
    kvf, bias, qf0, qf1, att0, att1, mid0, mid1, snd0, snd1, segs, inv_row, inv_ref, q_v, kv_v, keys, values, plan_row,
    kv_recv, q_recv, p1_send, mid_recv, mid_send, out_recv, out_send, small, group_in, all_in,
):
    rank, ctx = lax.axis_index("dp"), lax.axis_index("ctx")
    xs, zs = rank >> 3, rank & 7
    qf, att, mid, snd = (qf0, qf1), (att0, att1), (mid0, mid1), (snd0, snd1)
    my_rows = pl.ds(pl.multiple_of(ctx * ROWS, ROWS), ROWS)

    def kv_cols(i, g):
        return kv_v.at[i, :, pl.ds(pl.multiple_of(g * LANES, LANES), LANES)]

    def q_cols(i, g, c):
        return q_v.at[i, :, pl.ds(pl.multiple_of(g * 2 * LANES + c * LANES, LANES), LANES)]

    def remote(src, dst, send, recv, to):
        pltpu.make_async_remote_copy(
            src_ref=src, dst_ref=dst, send_sem=send, recv_sem=recv, device_id=to, device_id_type=MESH
        ).start()

    def await_bytes(ref, sem):
        pltpu.make_async_copy(ref, ref, sem).wait()

    def tell(sem, to):
        pl.semaphore_signal(sem, inc=1, device_id=to, device_id_type=MESH)

    def give_kv_q0(i):
        def one(n, _):
            g = (ctx + n) & 7
            remote(kv_cols(i, g), kvf.at[i, my_rows], p1_send.at[0], kv_recv.at[i], (rank, g))
            remote(q_cols(i, g, 0), qf0.at[i, my_rows], p1_send.at[1], q_recv.at[0, i], (rank, g))
            return 0

        for n in range(1, CTX):
            one(n, 0)

    def give_q1(i):
        def one(n, _):
            g = (ctx + n) & 7
            remote(q_cols(i, g, 1), qf1.at[i, my_rows], p1_send.at[2], q_recv.at[1, i], (rank, g))
            return 0

        for n in range(1, CTX):
            one(n, 0)

    barrier = pltpu.get_barrier_semaphore()

    @pl.when(ctx != 0)
    def _():
        tell(barrier, (rank, 0))

    first = pl.multiple_of((rank >> 1) * 2 * PACKS, 2 * PACKS)
    seg_copy = pltpu.make_async_copy(seg_ref.at[pl.ds(first, 2 * PACKS)], segs, small.at[0])
    seg_copy.start()
    plan_copy = pltpu.make_async_copy(plan_ref, plan_row, small.at[4])
    plan_copy.start()
    own = (pltpu.make_async_copy(kv_ref, kv_v, small.at[2]), pltpu.make_async_copy(q_ref, q_v, small.at[3]))
    for copy in own:
        copy.start()

    @pl.when(ctx == 0)
    def _():
        pl.semaphore_wait(barrier, CTX - 1)
        lax.fori_loop(1, CTX, lambda m, _: (tell(group_in, (rank, m)), 0)[1], 0)

    @pl.when(ctx != 0)
    def _():
        pl.semaphore_wait(group_in, 1)

    for copy in own:
        copy.wait()
    for i in range(AHEAD):
        give_kv_q0(i)
    for i in range(PACKS):
        pltpu.make_async_copy(kv_cols(i, ctx), kvf.at[i, my_rows], kv_recv.at[i]).start()
        for c in range(2):
            pltpu.make_async_copy(q_cols(i, ctx, c), qf[c].at[i, my_rows], q_recv.at[c, i]).start()

    @pl.when(ctx == 0)
    def _():
        lax.fori_loop(0, RANKS, lambda m, _: (tell(barrier, ((rank + m) & 31, 1)), 0)[1], 0)

    plan_copy.wait()
    place = jnp.transpose(jnp.broadcast_to(plan_row[...], (ALL, ALL)))
    wanted = lax.broadcasted_iota(jnp.int32, (ALL, ALL), 1)
    source = lax.broadcasted_iota(jnp.int32, (ALL, ALL), 0)
    inv_row[...] = jnp.max(jnp.where(place == wanted, source, 0), axis=0, keepdims=True)
    inv_copy = pltpu.make_async_copy(inv_row, inv_ref, small.at[1])
    inv_copy.start()
    seg_copy.wait()

    @pl.when(ctx == 1)
    def _():
        pl.semaphore_wait(barrier, RANKS)
        lax.fori_loop(1, CTX, lambda m, _: (tell(all_in, (rank, (1 + m) & 7)), 0)[1], 0)

    for i in range(PACKS):
        make_bias(segs, (rank & 1) * PACKS + i, bias, i)

    def far_first(k):
        return ZN // 2 + (1 - 2 * (k & 1)) * ((k + 1) >> 1)

    def spread(c, i):
        dst = mid[c].at[rank * PACKS + i]

        def ring(k, _):
            z = (zs + far_first(k)) & 7
            for m in range(XN):
                x = (xs + m) & 3
                block = ((z + ctx) & 7) * XN + x
                src = att[c].at[i, pl.ds(pl.multiple_of(block * SUB, SUB), SUB), :]
                if m:
                    remote(src, dst, mid_send.at[c], mid_recv.at[c], (x * ZN + z, ctx))
                else:

                    @pl.when(z == zs)
                    def _():
                        pltpu.make_async_copy(src, dst, mid_recv.at[c]).start()

                    @pl.when(z != zs)
                    def _():
                        remote(src, dst, mid_send.at[c], mid_recv.at[c], (x * ZN + z, ctx))

            return 0

        lax.fori_loop(0, ZN, ring, 0)

    for c in range(2):

        def work(i, _):
            if c == 0:
                await_bytes(kvf.at[i], kv_recv.at[i])
                prepare(kvf, keys, values, i)
            await_bytes(qf[c].at[i], q_recv.at[c, i])
            attend(qf[c], keys, values, bias, att[c], i)
            if c == 0:

                @pl.when((ctx != 1) & (i == 0))
                def _():
                    pl.semaphore_wait(all_in, 1)

            spread(c, i)
            later = i + AHEAD

            @pl.when(later < PACKS)
            def _():
                (give_kv_q0, give_q1)[c](later)

            if c == 0:

                @pl.when(later >= PACKS)
                def _():
                    give_q1(later - PACKS)

            return 0

        lax.fori_loop(0, PACKS, work, 0)

    inv_copy.wait()
    to_ctx = (zs + ctx) & 7

    for c in range(2):
        await_bytes(mid[c], mid_recv.at[c])

        dst = out_ref.at[
            :,
            pl.ds(pl.multiple_of(xs * SUB, SUB), SUB),
            pl.ds(pl.multiple_of(ctx * 2 * LANES + c * LANES, LANES), LANES),
        ]

        def deliver(k, _):
            z = (zs + far_first(k)) & 7
            for m in range(XN):
                to = ((xs + m) & 3) * ZN + z
                for j in range(PACKS):
                    snd[c][to * PACKS + j] = mid[c][inv_ref[0, to * PACKS + j]]
                src = snd[c].at[pl.ds(to * PACKS, PACKS)]
                if m:
                    remote(src, dst, out_send.at[c], out_recv, (to, to_ctx))
                else:
                    here = (z == zs) & (zs == 0)

                    @pl.when(here)
                    def _():
                        pltpu.make_async_copy(src, dst, out_recv).start()

                    @pl.when(jnp.logical_not(here))
                    def _():
                        remote(src, dst, out_send.at[c], out_recv, (to, to_ctx))

            return 0

        lax.fori_loop(0, ZN, deliver, 0)

    await_bytes(kvf.at[:, 0 : PACK - ROWS], p1_send.at[0])
    await_bytes(qf0.at[:, 0 : PACK - ROWS], p1_send.at[1])
    await_bytes(qf1.at[:, 0 : PACK - ROWS], p1_send.at[2])
    for c in range(2):
        await_bytes(mid[c].at[0 : ALL - PACKS], mid_send.at[c])

        @pl.when(zs == 0)
        def _():
            await_bytes(snd[c].at[0 : ALL - PACKS], out_send.at[c])

        @pl.when(zs != 0)
        def _():
            await_bytes(snd[c], out_send.at[c])

    await_bytes(out_ref, out_recv)


def per_device(queries, keyvals, segments, plan):
    full = (PACKS, PACK, LANES)
    pieces = (ALL, SUB, LANES)
    dma = pltpu.SemaphoreType.DMA
    return pl.pallas_call(
        kernel,
        out_shape=jax.ShapeDtypeStruct((PACKS, ROWS, queries.shape[2]), jnp.bfloat16),
        in_specs=[
            pl.BlockSpec(memory_space=pltpu.HBM),
            pl.BlockSpec(memory_space=pltpu.HBM),
            pl.BlockSpec(memory_space=pltpu.HBM),
            pl.BlockSpec(memory_space=pltpu.HBM),
        ],
        out_specs=pl.BlockSpec(memory_space=pl.ANY),
        scratch_shapes=[
            pltpu.VMEM(full, jnp.bfloat16),
            pltpu.VMEM((PACKS, PACK, WINDOW), jnp.float32),
            *[pltpu.VMEM(full, jnp.bfloat16)] * 4,
            *[pltpu.VMEM(pieces, jnp.bfloat16)] * 4,
            pltpu.VMEM((2 * PACKS, PACK), jnp.int32),
            pltpu.VMEM((1, ALL), jnp.int32),
            pltpu.SMEM((1, ALL), jnp.int32),
            pltpu.VMEM(queries.shape, jnp.bfloat16),
            pltpu.VMEM(keyvals.shape, jnp.bfloat16),
            *[pltpu.VMEM((2, PACKS, PACK, LANES), jnp.bfloat16)] * 2,
            pltpu.VMEM((1, ALL), jnp.int32),
            dma((PACKS,)),
            dma((2, PACKS)),
            dma((3,)),
            dma((2,)),
            dma((2,)),
            dma(()),
            dma((2,)),
            dma((5,)),
            pltpu.SemaphoreType.REGULAR,
            pltpu.SemaphoreType.REGULAR,
        ],
        compiler_params=pltpu.CompilerParams(collective_id=0, has_side_effects=True, vmem_limit_bytes=24 * 2**20),
        cost_estimate=pl.CostEstimate(flops=2 * 10**9, bytes_accessed=4 * 2**20, transcendentals=2 * 10**6),
    )(*(pltpu.with_memory_space_constraint(a, pltpu.HBM) for a in (plan.reshape(1, ALL), segments, queries, keyvals)))


def solution(mesh):
    return jax.shard_map(
        per_device,
        mesh=mesh,
        in_specs=(P("dp", "ctx", None), P("dp", "ctx", None), P(), P()),
        out_specs=P("dp", "ctx", None),
        check_vma=False,
    )
```

```python
import functools

import jax
import jax.numpy as jnp
from jax import lax
from jax.experimental import pallas as pl
from jax.experimental.pallas import tpu as pltpu
from jax.sharding import PartitionSpec as P

MESH = pl.DeviceIdType.MESH
HEAD = 64
PACK = 512
PACKS = 4
ALL = 128
XN, ZN, CTX = 4, 8, 8
RANKS = XN * ZN
AHEAD = 4
ROWS = PACK // CTX
SUB = ROWS // XN
LANES = 128
QB = 128
WINDOW = 384
NEG = -1e30
EXP2_SCALE = HEAD**-0.5 * 1.4426950408889634
NN = (((1,), (0,)), ((), ()))
NT = (((1,), (1,)), ((), ()))


def make_bias(seg_ref, row, bias, i):
    seg_row = seg_ref[pl.ds(row, 1), :]
    lower = lax.broadcasted_iota(jnp.int32, (QB, QB), 1) <= lax.broadcasted_iota(jnp.int32, (QB, QB), 0)
    for b in range(PACK // QB):
        seg_q = jnp.transpose(jnp.broadcast_to(seg_row[:, b * QB : (b + 1) * QB], (QB, QB)))
        first = max(0, b - 2)
        for kb in range(first, b + 1):
            seg_k = jnp.broadcast_to(seg_row[:, kb * QB : (kb + 1) * QB], (QB, QB))
            same = seg_q == seg_k
            if kb == b:
                same = same & lower
            bias[i, b * QB : (b + 1) * QB, (kb - first) * QB : (kb - first + 1) * QB] = jnp.where(same, 0.0, NEG)


def prepare(kvf, keys, values, i):
    kv = kvf[i].astype(jnp.float32)
    swapped = pltpu.roll(kv, HEAD, 1)
    left = lax.broadcasted_iota(jnp.int32, (PACK, LANES), 1) < HEAD
    keys[i] = jnp.where(left, kv, 0.0).astype(jnp.bfloat16)
    values[i] = jnp.where(left, swapped, 1.0).astype(jnp.bfloat16)


def attend(q_c, keys, values, bias, att_c, i):
    left = lax.broadcasted_iota(jnp.int32, (QB, LANES), 1) < HEAD
    left_two = lax.broadcasted_iota(jnp.int32, (2 * QB, LANES), 1) < HEAD
    for b in range(PACK // QB):
        lo, hi = max(0, b - 2) * QB, (b + 1) * QB
        q = q_c[i, b * QB : hi, :]
        other = pltpu.roll(q.astype(jnp.float32), HEAD, 1).astype(jnp.bfloat16)
        both = jnp.concatenate([q, other], axis=0)
        s = lax.dot_general(both, keys[i, lo:hi, :], NT, preferred_element_type=jnp.float32)
        mask = bias[i, b * QB : hi, 0 : hi - lo]
        s = (s.reshape(2, QB, hi - lo) + mask[None]).reshape(2 * QB, hi - lo)
        top = jnp.max(s, axis=1, keepdims=True)
        p = jnp.exp2((s - top) * EXP2_SCALE).astype(jnp.bfloat16)
        sums = lax.dot_general(p, values[i, lo:hi, :], NN, preferred_element_type=jnp.float32)
        norm = jnp.where(left_two, pltpu.roll(sums, HEAD, 1), 1.0)
        mixed = sums / norm
        out = jnp.where(left, mixed[:QB], pltpu.roll(mixed[QB:], HEAD, 1))
        att_c[i, b * QB : hi, :] = out.astype(jnp.bfloat16)


def kernel(
    plan_ref, seg_ref, q_ref, kv_ref, out_ref,
    kvf, bias, qf0, qf1, att0, att1, mid0, mid1, snd0, snd1, segs, inv_row, inv_ref, q_v, kv_v, keys, values, plan_row,
    kv_recv, q_recv, p1_send, mid_recv, mid_send, out_recv, out_send, small, group_in, all_in,
):
    rank, ctx = lax.axis_index("dp"), lax.axis_index("ctx")
    xs, zs = rank >> 3, rank & 7
    qf, att, mid, snd = (qf0, qf1), (att0, att1), (mid0, mid1), (snd0, snd1)
    my_rows = pl.ds(pl.multiple_of(ctx * ROWS, ROWS), ROWS)

    def kv_cols(i, g):
        return kv_v.at[i, :, pl.ds(pl.multiple_of(g * LANES, LANES), LANES)]

    def q_cols(i, g, c):
        return q_v.at[i, :, pl.ds(pl.multiple_of(g * 2 * LANES + c * LANES, LANES), LANES)]

    def remote(src, dst, send, recv, to):
        pltpu.make_async_remote_copy(
            src_ref=src, dst_ref=dst, send_sem=send, recv_sem=recv, device_id=to, device_id_type=MESH
        ).start()

    def await_bytes(ref, sem):
        pltpu.make_async_copy(ref, ref, sem).wait()

    def tell(sem, to):
        pl.semaphore_signal(sem, inc=1, device_id=to, device_id_type=MESH)

    def give_kv_q0(i):
        def one(n, _):
            g = (ctx + n) & 7
            remote(kv_cols(i, g), kvf.at[i, my_rows], p1_send.at[0], kv_recv.at[i], (rank, g))
            remote(q_cols(i, g, 0), qf0.at[i, my_rows], p1_send.at[1], q_recv.at[0, i], (rank, g))
            return 0

        for n in range(1, CTX):
            one(n, 0)

    def give_q1(i):
        def one(n, _):
            g = (ctx + n) & 7
            remote(q_cols(i, g, 1), qf1.at[i, my_rows], p1_send.at[2], q_recv.at[1, i], (rank, g))
            return 0

        for n in range(1, CTX):
            one(n, 0)

    barrier = pltpu.get_barrier_semaphore()

    @pl.when(ctx != 0)
    def _():
        tell(barrier, (rank, 0))

    first = pl.multiple_of((rank >> 1) * 2 * PACKS, 2 * PACKS)
    seg_copy = pltpu.make_async_copy(seg_ref.at[pl.ds(first, 2 * PACKS)], segs, small.at[0])
    seg_copy.start()
    plan_copy = pltpu.make_async_copy(plan_ref, plan_row, small.at[4])
    plan_copy.start()
    own = (pltpu.make_async_copy(kv_ref, kv_v, small.at[2]), pltpu.make_async_copy(q_ref, q_v, small.at[3]))
    for copy in own:
        copy.start()

    @pl.when(ctx == 0)
    def _():
        pl.semaphore_wait(barrier, CTX - 1)
        lax.fori_loop(1, CTX, lambda m, _: (tell(group_in, (rank, m)), 0)[1], 0)

    @pl.when(ctx != 0)
    def _():
        pl.semaphore_wait(group_in, 1)

    for copy in own:
        copy.wait()
    for i in range(AHEAD):
        give_kv_q0(i)
    for i in range(PACKS):
        pltpu.make_async_copy(kv_cols(i, ctx), kvf.at[i, my_rows], kv_recv.at[i]).start()
        for c in range(2):
            pltpu.make_async_copy(q_cols(i, ctx, c), qf[c].at[i, my_rows], q_recv.at[c, i]).start()

    @pl.when(ctx == 0)
    def _():
        lax.fori_loop(0, RANKS, lambda m, _: (tell(barrier, ((rank + m) & 31, 1)), 0)[1], 0)

    plan_copy.wait()
    place = jnp.transpose(jnp.broadcast_to(plan_row[...], (ALL, ALL)))
    wanted = lax.broadcasted_iota(jnp.int32, (ALL, ALL), 1)
    source = lax.broadcasted_iota(jnp.int32, (ALL, ALL), 0)
    inv_row[...] = jnp.max(jnp.where(place == wanted, source, 0), axis=0, keepdims=True)
    inv_copy = pltpu.make_async_copy(inv_row, inv_ref, small.at[1])
    inv_copy.start()
    seg_copy.wait()

    @pl.when(ctx == 1)
    def _():
        pl.semaphore_wait(barrier, RANKS)
        lax.fori_loop(1, CTX, lambda m, _: (tell(all_in, (rank, (1 + m) & 7)), 0)[1], 0)

    for i in range(PACKS):
        make_bias(segs, (rank & 1) * PACKS + i, bias, i)

    def far_first(k):
        return ZN // 2 + (1 - 2 * (k & 1)) * ((k + 1) >> 1)

    def spread(c, i):
        dst = mid[c].at[rank * PACKS + i]

        def ring(k, _):
            z = (zs + far_first(k)) & 7
            for m in range(XN):
                x = (xs + m) & 3
                block = ((z + ctx) & 7) * XN + x
                src = att[c].at[i, pl.ds(pl.multiple_of(block * SUB, SUB), SUB), :]
                if m:
                    remote(src, dst, mid_send.at[c], mid_recv.at[c], (x * ZN + z, ctx))
                else:

                    @pl.when(z == zs)
                    def _():
                        pltpu.make_async_copy(src, dst, mid_recv.at[c]).start()

                    @pl.when(z != zs)
                    def _():
                        remote(src, dst, mid_send.at[c], mid_recv.at[c], (x * ZN + z, ctx))

            return 0

        lax.fori_loop(0, ZN, ring, 0)

    for c in range(2):

        def work(i, _):
            if c == 0:
                await_bytes(kvf.at[i], kv_recv.at[i])
                prepare(kvf, keys, values, i)
            await_bytes(qf[c].at[i], q_recv.at[c, i])
            attend(qf[c], keys, values, bias, att[c], i)
            if c == 0:

                @pl.when((ctx != 1) & (i == 0))
                def _():
                    pl.semaphore_wait(all_in, 1)

            spread(c, i)
            later = i + AHEAD

            @pl.when(later < PACKS)
            def _():
                (give_kv_q0, give_q1)[c](later)

            if c == 0:

                @pl.when(later >= PACKS)
                def _():
                    give_q1(later - PACKS)

            return 0

        lax.fori_loop(0, PACKS, work, 0)

    inv_copy.wait()
    to_ctx = (zs + ctx) & 7

    for c in range(2):
        await_bytes(mid[c], mid_recv.at[c])

        dst = out_ref.at[
            :,
            pl.ds(pl.multiple_of(xs * SUB, SUB), SUB),
            pl.ds(pl.multiple_of(ctx * 2 * LANES + c * LANES, LANES), LANES),
        ]

        def deliver(k, _):
            z = (zs + far_first(k)) & 7
            for m in range(XN):
                to = ((xs + m) & 3) * ZN + z
                for j in range(PACKS):
                    snd[c][to * PACKS + j] = mid[c][inv_ref[0, to * PACKS + j]]
                src = snd[c].at[pl.ds(to * PACKS, PACKS)]
                if m:
                    remote(src, dst, out_send.at[c], out_recv, (to, to_ctx))
                else:
                    here = (z == zs) & (zs == 0)

                    @pl.when(here)
                    def _():
                        pltpu.make_async_copy(src, dst, out_recv).start()

                    @pl.when(jnp.logical_not(here))
                    def _():
                        remote(src, dst, out_send.at[c], out_recv, (to, to_ctx))

            return 0

        lax.fori_loop(0, ZN, deliver, 0)

    await_bytes(kvf.at[:, 0 : PACK - ROWS], p1_send.at[0])
    await_bytes(qf0.at[:, 0 : PACK - ROWS], p1_send.at[1])
    await_bytes(qf1.at[:, 0 : PACK - ROWS], p1_send.at[2])
    for c in range(2):
        await_bytes(mid[c].at[0 : ALL - PACKS], mid_send.at[c])

        @pl.when(zs == 0)
        def _():
            await_bytes(snd[c].at[0 : ALL - PACKS], out_send.at[c])

        @pl.when(zs != 0)
        def _():
            await_bytes(snd[c], out_send.at[c])

    await_bytes(out_ref, out_recv)


def per_device(queries, keyvals, segments, plan):
    full = (PACKS, PACK, LANES)
    pieces = (ALL, SUB, LANES)
    dma = pltpu.SemaphoreType.DMA
    return pl.pallas_call(
        kernel,
        out_shape=jax.ShapeDtypeStruct((PACKS, ROWS, queries.shape[2]), jnp.bfloat16),
        in_specs=[
            pl.BlockSpec(memory_space=pltpu.HBM),
            pl.BlockSpec(memory_space=pltpu.HBM),
            pl.BlockSpec(memory_space=pltpu.HBM),
            pl.BlockSpec(memory_space=pltpu.HBM),
        ],
        out_specs=pl.BlockSpec(memory_space=pl.ANY),
        scratch_shapes=[
            pltpu.VMEM(full, jnp.bfloat16),
            pltpu.VMEM((PACKS, PACK, WINDOW), jnp.float32),
            *[pltpu.VMEM(full, jnp.bfloat16)] * 4,
            *[pltpu.VMEM(pieces, jnp.bfloat16)] * 4,
            pltpu.VMEM((2 * PACKS, PACK), jnp.int32),
            pltpu.VMEM((1, ALL), jnp.int32),
            pltpu.SMEM((1, ALL), jnp.int32),
            pltpu.VMEM(queries.shape, jnp.bfloat16),
            pltpu.VMEM(keyvals.shape, jnp.bfloat16),
            *[pltpu.VMEM(full, jnp.bfloat16)] * 2,
            pltpu.VMEM((1, ALL), jnp.int32),
            dma((PACKS,)),
            dma((2, PACKS)),
            dma((3,)),
            dma((2,)),
            dma((2,)),
            dma(()),
            dma((2,)),
            dma((5,)),
            pltpu.SemaphoreType.REGULAR,
            pltpu.SemaphoreType.REGULAR,
        ],
        compiler_params=pltpu.CompilerParams(collective_id=0, has_side_effects=True, vmem_limit_bytes=24 * 2**20),
        cost_estimate=pl.CostEstimate(flops=2 * 10**9, bytes_accessed=4 * 2**20, transcendentals=2 * 10**6),
    )(*(pltpu.with_memory_space_constraint(a, pltpu.HBM) for a in (plan.reshape(1, ALL), segments, queries, keyvals)))


def solution(mesh):
    return jax.shard_map(
        per_device,
        mesh=mesh,
        in_specs=(P("dp", "ctx", None), P("dp", "ctx", None), P(), P()),
        out_specs=P("dp", "ctx", None),
        check_vma=False,
    )
```

```python
import functools

import jax
import jax.numpy as jnp
from jax import lax
from jax.experimental import pallas as pl
from jax.experimental.pallas import tpu as pltpu
from jax.sharding import PartitionSpec as P

MESH = pl.DeviceIdType.MESH
HEAD = 64
PACK = 512
PACKS = 4
ALL = 128
XN, ZN, CTX = 4, 8, 8
RANKS = XN * ZN
AHEAD = 4
ROWS = PACK // CTX
SUB = ROWS // XN
LANES = 128
QB = 128
WINDOW = 384
NEG = -1e30
EXP2_SCALE = HEAD**-0.5 * 1.4426950408889634
NN = (((1,), (0,)), ((), ()))
NT = (((1,), (1,)), ((), ()))


def make_bias(seg_ref, row, bias, i):
    seg_row = seg_ref[pl.ds(row, 1), :]
    lower = lax.broadcasted_iota(jnp.int32, (QB, QB), 1) <= lax.broadcasted_iota(jnp.int32, (QB, QB), 0)
    for b in range(PACK // QB):
        seg_q = jnp.transpose(jnp.broadcast_to(seg_row[:, b * QB : (b + 1) * QB], (QB, QB)))
        first = max(0, b - 2)
        for kb in range(first, b + 1):
            seg_k = jnp.broadcast_to(seg_row[:, kb * QB : (kb + 1) * QB], (QB, QB))
            same = seg_q == seg_k
            if kb == b:
                same = same & lower
            bias[i, b * QB : (b + 1) * QB, (kb - first) * QB : (kb - first + 1) * QB] = jnp.where(same, 0.0, NEG)


def prepare(kvf, keys, values, i):
    kv = kvf[i].astype(jnp.float32)
    swapped = pltpu.roll(kv, HEAD, 1)
    left = lax.broadcasted_iota(jnp.int32, (PACK, LANES), 1) < HEAD
    keys[i] = jnp.where(left, kv, 0.0).astype(jnp.bfloat16)
    values[i] = jnp.where(left, swapped, 1.0).astype(jnp.bfloat16)


def attend(q_c, keys, values, bias, att_c, i):
    left = lax.broadcasted_iota(jnp.int32, (QB, LANES), 1) < HEAD
    for b in range(PACK // QB):
        lo, hi = max(0, b - 2) * QB, (b + 1) * QB
        q = q_c[i, b * QB : hi, :]
        other = pltpu.roll(q.astype(jnp.float32), HEAD, 1).astype(jnp.bfloat16)
        both = jnp.concatenate([q, other], axis=0)
        s = lax.dot_general(both, keys[i, lo:hi, :], NT, preferred_element_type=jnp.float32)
        mask = bias[i, b * QB : hi, 0 : hi - lo]
        s = (s.reshape(2, QB, hi - lo) + mask[None]).reshape(2 * QB, hi - lo)
        top = jnp.max(s, axis=1, keepdims=True)
        p = jnp.exp2((s - top) * EXP2_SCALE).astype(jnp.bfloat16)
        sums = lax.dot_general(p, values[i, lo:hi, :], NN, preferred_element_type=jnp.float32)
        one, two = sums[:QB], sums[QB:]
        out = jnp.where(left, one, pltpu.roll(two, HEAD, 1)) / jnp.where(left, pltpu.roll(one, HEAD, 1), two)
        att_c[i, b * QB : hi, :] = out.astype(jnp.bfloat16)


def kernel(
    plan_ref, seg_ref, q_ref, kv_ref, out_ref,
    kvf, bias, qf0, qf1, att0, att1, mid0, mid1, snd0, snd1, segs, inv_row, inv_ref, q_v, kv_v, keys, values, plan_row,
    kv_recv, q_recv, p1_send, mid_recv, mid_send, out_recv, out_send, small, group_in, all_in,
):
    rank, ctx = lax.axis_index("dp"), lax.axis_index("ctx")
    xs, zs = rank >> 3, rank & 7
    qf, att, mid, snd = (qf0, qf1), (att0, att1), (mid0, mid1), (snd0, snd1)
    my_rows = pl.ds(pl.multiple_of(ctx * ROWS, ROWS), ROWS)

    def kv_cols(i, g):
        return kv_v.at[i, :, pl.ds(pl.multiple_of(g * LANES, LANES), LANES)]

    def q_cols(i, g, c):
        return q_v.at[i, :, pl.ds(pl.multiple_of(g * 2 * LANES + c * LANES, LANES), LANES)]

    def remote(src, dst, send, recv, to):
        pltpu.make_async_remote_copy(
            src_ref=src, dst_ref=dst, send_sem=send, recv_sem=recv, device_id=to, device_id_type=MESH
        ).start()

    def await_bytes(ref, sem):
        pltpu.make_async_copy(ref, ref, sem).wait()

    def tell(sem, to):
        pl.semaphore_signal(sem, inc=1, device_id=to, device_id_type=MESH)

    def give_kv_q0(i):
        def one(n, _):
            g = (ctx + n) & 7
            remote(kv_cols(i, g), kvf.at[i, my_rows], p1_send.at[0], kv_recv.at[i], (rank, g))
            remote(q_cols(i, g, 0), qf0.at[i, my_rows], p1_send.at[1], q_recv.at[0, i], (rank, g))
            return 0

        for n in range(1, CTX):
            one(n, 0)

    def give_q1(i):
        def one(n, _):
            g = (ctx + n) & 7
            remote(q_cols(i, g, 1), qf1.at[i, my_rows], p1_send.at[2], q_recv.at[1, i], (rank, g))
            return 0

        for n in range(1, CTX):
            one(n, 0)

    barrier = pltpu.get_barrier_semaphore()

    @pl.when(ctx != 0)
    def _():
        tell(barrier, (rank, 0))

    first = pl.multiple_of((rank >> 1) * 2 * PACKS, 2 * PACKS)
    seg_copy = pltpu.make_async_copy(seg_ref.at[pl.ds(first, 2 * PACKS)], segs, small.at[0])
    seg_copy.start()
    plan_copy = pltpu.make_async_copy(plan_ref, plan_row, small.at[4])
    plan_copy.start()
    own = (pltpu.make_async_copy(kv_ref, kv_v, small.at[2]), pltpu.make_async_copy(q_ref, q_v, small.at[3]))
    for copy in own:
        copy.start()

    @pl.when(ctx == 0)
    def _():
        pl.semaphore_wait(barrier, CTX - 1)
        lax.fori_loop(1, CTX, lambda m, _: (tell(group_in, (rank, m)), 0)[1], 0)

    @pl.when(ctx != 0)
    def _():
        pl.semaphore_wait(group_in, 1)

    for copy in own:
        copy.wait()
    for i in range(AHEAD):
        give_kv_q0(i)
    for i in range(PACKS):
        pltpu.make_async_copy(kv_cols(i, ctx), kvf.at[i, my_rows], kv_recv.at[i]).start()
        for c in range(2):
            pltpu.make_async_copy(q_cols(i, ctx, c), qf[c].at[i, my_rows], q_recv.at[c, i]).start()

    @pl.when(ctx == 0)
    def _():
        lax.fori_loop(0, RANKS, lambda m, _: (tell(barrier, ((rank + m) & 31, 1)), 0)[1], 0)

    plan_copy.wait()
    place = jnp.transpose(jnp.broadcast_to(plan_row[...], (ALL, ALL)))
    wanted = lax.broadcasted_iota(jnp.int32, (ALL, ALL), 1)
    source = lax.broadcasted_iota(jnp.int32, (ALL, ALL), 0)
    inv_row[...] = jnp.max(jnp.where(place == wanted, source, 0), axis=0, keepdims=True)
    inv_copy = pltpu.make_async_copy(inv_row, inv_ref, small.at[1])
    inv_copy.start()
    seg_copy.wait()

    @pl.when(ctx == 1)
    def _():
        pl.semaphore_wait(barrier, RANKS)
        lax.fori_loop(1, CTX, lambda m, _: (tell(all_in, (rank, (1 + m) & 7)), 0)[1], 0)

    for i in range(PACKS):
        make_bias(segs, (rank & 1) * PACKS + i, bias, i)

    def far_first(k):
        return ZN // 2 + (1 - 2 * (k & 1)) * ((k + 1) >> 1)

    def spread(c, i):
        dst = mid[c].at[rank * PACKS + i]

        def ring(k, _):
            z = (zs + far_first(k)) & 7
            for m in range(XN):
                x = (xs + m) & 3
                block = ((z + ctx) & 7) * XN + x
                src = att[c].at[i, pl.ds(pl.multiple_of(block * SUB, SUB), SUB), :]
                if m:
                    remote(src, dst, mid_send.at[c], mid_recv.at[c], (x * ZN + z, ctx))
                else:

                    @pl.when(z == zs)
                    def _():
                        pltpu.make_async_copy(src, dst, mid_recv.at[c]).start()

                    @pl.when(z != zs)
                    def _():
                        remote(src, dst, mid_send.at[c], mid_recv.at[c], (x * ZN + z, ctx))

            return 0

        lax.fori_loop(0, ZN, ring, 0)

    for c in range(2):

        def work(i, _):
            if c == 0:
                await_bytes(kvf.at[i], kv_recv.at[i])
                prepare(kvf, keys, values, i)
            await_bytes(qf[c].at[i], q_recv.at[c, i])
            attend(qf[c], keys, values, bias, att[c], i)
            if c == 0:

                @pl.when((ctx != 1) & (i == 0))
                def _():
                    pl.semaphore_wait(all_in, 1)

            spread(c, i)
            later = i + AHEAD

            @pl.when(later < PACKS)
            def _():
                (give_kv_q0, give_q1)[c](later)

            if c == 0:

                @pl.when(later >= PACKS)
                def _():
                    give_q1(later - PACKS)

            return 0

        lax.fori_loop(0, PACKS, work, 0)

    inv_copy.wait()
    to_ctx = (zs + ctx) & 7

    for c in range(2):
        await_bytes(mid[c], mid_recv.at[c])

        dst = out_ref.at[
            :,
            pl.ds(pl.multiple_of(xs * SUB, SUB), SUB),
            pl.ds(pl.multiple_of(ctx * 2 * LANES + c * LANES, LANES), LANES),
        ]

        def deliver(k, _):
            z = (zs + far_first(k)) & 7
            for m in range(XN):
                to = ((xs + m) & 3) * ZN + z
                for j in range(PACKS):
                    snd[c][to * PACKS + j] = mid[c][inv_ref[0, to * PACKS + j]]
                src = snd[c].at[pl.ds(to * PACKS, PACKS)]
                if m:
                    remote(src, dst, out_send.at[c], out_recv, (to, to_ctx))
                else:
                    here = (z == zs) & (zs == 0)

                    @pl.when(here)
                    def _():
                        pltpu.make_async_copy(src, dst, out_recv).start()

                    @pl.when(jnp.logical_not(here))
                    def _():
                        remote(src, dst, out_send.at[c], out_recv, (to, to_ctx))

            return 0

        lax.fori_loop(0, ZN, deliver, 0)

    await_bytes(kvf.at[:, 0 : PACK - ROWS], p1_send.at[0])
    await_bytes(qf0.at[:, 0 : PACK - ROWS], p1_send.at[1])
    await_bytes(qf1.at[:, 0 : PACK - ROWS], p1_send.at[2])
    for c in range(2):
        await_bytes(mid[c].at[0 : ALL - PACKS], mid_send.at[c])

        @pl.when(zs == 0)
        def _():
            await_bytes(snd[c].at[0 : ALL - PACKS], out_send.at[c])

        @pl.when(zs != 0)
        def _():
            await_bytes(snd[c], out_send.at[c])

    await_bytes(out_ref, out_recv)


def per_device(queries, keyvals, segments, plan):
    full = (PACKS, PACK, LANES)
    pieces = (ALL, SUB, LANES)
    dma = pltpu.SemaphoreType.DMA
    return pl.pallas_call(
        kernel,
        out_shape=jax.ShapeDtypeStruct((PACKS, ROWS, queries.shape[2]), jnp.bfloat16),
        in_specs=[
            pl.BlockSpec(memory_space=pltpu.HBM),
            pl.BlockSpec(memory_space=pltpu.HBM),
            pl.BlockSpec(memory_space=pltpu.HBM),
            pl.BlockSpec(memory_space=pltpu.HBM),
        ],
        out_specs=pl.BlockSpec(memory_space=pl.ANY),
        scratch_shapes=[
            pltpu.VMEM(full, jnp.bfloat16),
            pltpu.VMEM((PACKS, PACK, WINDOW), jnp.float32),
            *[pltpu.VMEM(full, jnp.bfloat16)] * 4,
            *[pltpu.VMEM(pieces, jnp.bfloat16)] * 4,
            pltpu.VMEM((2 * PACKS, PACK), jnp.int32),
            pltpu.VMEM((1, ALL), jnp.int32),
            pltpu.SMEM((1, ALL), jnp.int32),
            pltpu.VMEM(queries.shape, jnp.bfloat16),
            pltpu.VMEM(keyvals.shape, jnp.bfloat16),
            *[pltpu.VMEM(full, jnp.bfloat16)] * 2,
            pltpu.VMEM((1, ALL), jnp.int32),
            dma((PACKS,)),
            dma((2, PACKS)),
            dma((3,)),
            dma((2,)),
            dma((2,)),
            dma(()),
            dma((2,)),
            dma((5,)),
            pltpu.SemaphoreType.REGULAR,
            pltpu.SemaphoreType.REGULAR,
        ],
        compiler_params=pltpu.CompilerParams(collective_id=0, has_side_effects=True, vmem_limit_bytes=24 * 2**20),
        cost_estimate=pl.CostEstimate(flops=2 * 10**9, bytes_accessed=4 * 2**20, transcendentals=2 * 10**6),
    )(*(pltpu.with_memory_space_constraint(a, pltpu.HBM) for a in (plan.reshape(1, ALL), segments, queries, keyvals)))


def solution(mesh):
    return jax.shard_map(
        per_device,
        mesh=mesh,
        in_specs=(P("dp", "ctx", None), P("dp", "ctx", None), P(), P()),
        out_specs=P("dp", "ctx", None),
        check_vma=False,
    )
```
